32 devices in a mesh: groups: 2 (over x), tensor: 16 (over z, y, core).
Axes of the slice: x: 2, y: 2, z: 4, core: 2. Of those that a mesh axis runs over, the one named last changes fastest.
Arguments:
- queries: bfloat16 [512, 16384], P('groups', 'tensor'), parts along dimension 0, may hold values from -7 to 7
- keys: bfloat16 [4096, 1024], P(('groups', 'tensor')), parts along dimension 0, may hold values from -6 to 6
- values: bfloat16 [4096, 1024], P(('groups', 'tensor')), parts along dimension 0, may hold values from -6 to 6
- lengths: int32 [32], P(('groups', 'tensor')), parts along dimension 0, may hold values from 64 to 128, as said below
- start_pos: int32 [2], P('groups'), parts along dimension 0, may hold values from 512 to 1792
- out_weight: bfloat16 [16384, 16384], P('tensor'), may hold values from -0.046875 to 0.046875
Outputs:
- layer_output: bfloat16 [512, 16384], P('groups'), parts along dimension 0
The draws below stay inside these ranges and needn't reach their ends.
There are 2 independent parts, one for each index of `groups`. The reference program is written for one: setup_inputs(seed, part) draws one part's arguments, and reference() takes and returns one part's arrays. A program takes and returns all parts, laid end to end along the dimension named above; an argument that names none is the same for every part. Nothing has to cross between parts.
Inputs may be any that keep to these rules, and one draw needn't show every extreme that they name: `lengths`: each shard's prefix is at least half of its 128 slots; some shard is full and some holds exactly half.
All inputs are finite; a program needn't handle non-finite values.
Results may differ from the reference program's by a relative error of at most 0.014.
Values may be sent and summed in bfloat16 or wider, within the bound.
No kernel may reach another device: no remote copies, remote signals or barrier semaphores. Data moves between devices by JAX's collectives and lax.ppermute only.
A program may use at most 128 MiB of HBM per device.

```python
import jax
import jax.numpy as jnp
from jax import lax

D = 16384
HEADS = 128
KV_HEADS = 8
HEAD_DIM = 128
TOK = 256
CTX_DEV = 128
CTX = 2048
N_TENSOR = 16


def draw_keys(key, part):
    key = jax.random.fold_in(key, 11)
    drawn = jnp.clip(jax.random.normal(key, (CTX, KV_HEADS * HEAD_DIM), jnp.float32), -6.0, 6.0)
    return drawn.astype(jnp.bfloat16)


def draw_queries(key, part):
    key = jax.random.fold_in(key, 23)
    drawn = jnp.clip(jax.random.normal(key, (TOK, HEADS * HEAD_DIM), jnp.float32), -6.0, 6.0)
    return drawn.astype(jnp.bfloat16)


def draw_lengths(key, part):
    key = jax.random.fold_in(key, 37)
    shard_count = CTX // CTX_DEV
    key_fill, key_order = jax.random.split(key)
    filled = jax.random.randint(key_fill, (shard_count,), CTX_DEV // 2, CTX_DEV + 1, jnp.int32)
    order = jax.random.permutation(key_order, shard_count)
    filled = filled.at[order[0]].set(CTX_DEV)
    filled = filled.at[order[1]].set(CTX_DEV // 2)
    return filled


def block_scale(stream_key, shape, cuts, smallest, high):
    factor_of, own = 1.0, jax.random.fold_in(stream_key, 6)
    for dim, shards_of in cuts:
        heights = jnp.exp(jax.random.uniform(jax.random.fold_in(own, dim), (shards_of,), jnp.float32, smallest / len(cuts), high / len(cuts)))
        factor_of = factor_of * jnp.repeat(heights, shape[dim] // shards_of).reshape([-1 if axis == dim else 1 for axis in range(len(shape))])
    return factor_of


def scatter_about(key, shape, width, limit, shards=(), kind=jnp.bfloat16):
    array = width * jax.random.normal(key, shape, jnp.float32)
    if shards:
        array = array * block_scale(key, shape, shards, -0.22, 0.18)
    return jnp.clip(array, -limit, limit).astype(kind)


def setup_inputs(seed: int = 0, part: int = 0) -> dict:
    streams_of = jax.random.split(jax.random.key(seed), 7)
    part_splits = jax.random.split(jax.random.fold_in(streams_of[6], part), 7)
    return {
        "queries": draw_queries(jax.random.fold_in(jax.random.fold_in(streams_of[6], part), 71), part),
        "keys": draw_keys(jax.random.fold_in(jax.random.fold_in(streams_of[6], part), 71), part),
        "values": scatter_about(part_splits[2], (CTX, KV_HEADS * HEAD_DIM), 1.0, 6.0, ((0, 16),)),
        "lengths": draw_lengths(jax.random.fold_in(jax.random.fold_in(streams_of[6], part), 71), part),
        "start_pos": jax.random.randint(part_splits[4], (1,), CTX // 4, CTX - TOK + 1).astype(jnp.int32),
        "out_weight": scatter_about(streams_of[5], (HEADS * HEAD_DIM, D), (HEADS * HEAD_DIM) ** -0.5, 0.046875, ((0, 16),)),
    }


def reference(queries, keys, values, lengths, start_pos, out_weight):
    group_size = HEADS // KV_HEADS
    positions = jnp.arange(CTX, dtype=jnp.int32)
    shard_index = positions // CTX_DEV
    local_index = positions % CTX_DEV
    live_slot = local_index < lengths[shard_index]
    query_pos = start_pos[0] + jnp.arange(TOK, dtype=jnp.int32)
    visible = live_slot[None, :] & (positions[None, :] <= query_pos[:, None])
    score_scale = HEAD_DIM ** -0.5

    def one_head(head):
        kv_head = head // group_size
        query_rows = lax.dynamic_slice_in_dim(queries, head * HEAD_DIM, HEAD_DIM, 1)
        key_rows = lax.dynamic_slice_in_dim(keys, kv_head * HEAD_DIM, HEAD_DIM, 1)
        value_rows = lax.dynamic_slice_in_dim(values, kv_head * HEAD_DIM, HEAD_DIM, 1)
        scores = jnp.dot(query_rows, key_rows.T, preferred_element_type=jnp.float32) * score_scale
        scores = jnp.where(visible, scores, -1e30)
        top_score = jnp.max(scores, axis=-1, keepdims=True)
        raw_weights = jnp.where(visible, jnp.exp(scores - top_score), 0.0)
        row_total = jnp.sum(raw_weights, axis=-1, keepdims=True)
        mixed = jnp.dot(raw_weights.astype(jnp.bfloat16), value_rows, preferred_element_type=jnp.float32)
        return mixed / row_total

    head_outputs = lax.map(one_head, jnp.arange(HEADS, dtype=jnp.int32))
    attended = jnp.transpose(head_outputs, (1, 0, 2)).reshape(TOK, HEADS * HEAD_DIM).astype(jnp.bfloat16)
    head_width = HEADS * HEAD_DIM // N_TENSOR

    def add_device(running_sum, device):
        attended_cols = lax.dynamic_slice_in_dim(attended, device * head_width, head_width, 1)
        weight_rows = lax.dynamic_slice_in_dim(out_weight, device * head_width, head_width, 0)
        partial_value = jnp.dot(attended_cols, weight_rows, preferred_element_type=jnp.float32).astype(jnp.bfloat16)
        kept = lax.optimization_barrier(partial_value)
        return running_sum + kept.astype(jnp.float32), None

    summed, _ = lax.scan(add_device, jnp.zeros((TOK, D), jnp.float32), jnp.arange(N_TENSOR, dtype=jnp.int32))
    return summed.astype(jnp.bfloat16)
```

```python
import functools
import math

import jax
import jax.numpy as jnp
from jax import lax
from jax.experimental import pallas as pl
from jax.experimental.pallas import tpu as pltpu
from jax.sharding import PartitionSpec as P

HEADS = 128
KV_HEADS = 8
HEAD_DIM = 128
GROUP = HEADS // KV_HEADS
FLAG_ROWS = 16
CHUNKS = 8
BLOCK_COLS = 512
SLOTS = 8
VMEM_LIMIT = 32 * 1024 * 1024


def pack_kernel(heads_ref, lengths_ref, k_ref, v_ref, *out_refs):
    slots = k_ref.shape[0]
    length = jnp.full((FLAG_ROWS, HEAD_DIM), lengths_ref[0], jnp.int32)
    length = length.astype(jnp.float32).astype(jnp.bfloat16)
    for m, out in enumerate(out_refs):
        cols = pl.ds(pl.multiple_of(heads_ref[m] * HEAD_DIM, HEAD_DIM), HEAD_DIM)
        out[:slots, :] = k_ref[:, cols]
        out[slots : 2 * slots, :] = v_ref[:, cols]
        out[2 * slots :, :] = length


def pack(heads, lengths, keys, values):
    slots = keys.shape[0]
    piece = jax.ShapeDtypeStruct((2 * slots + FLAG_ROWS, HEAD_DIM), jnp.bfloat16)
    smem = pl.BlockSpec(memory_space=pltpu.SMEM)
    vmem = pl.BlockSpec(memory_space=pltpu.VMEM)
    return pl.pallas_call(
        pack_kernel,
        out_shape=[piece] * heads.shape[0],
        in_specs=[smem, smem, vmem, vmem],
        out_specs=[vmem] * heads.shape[0],
        compiler_params=pltpu.CompilerParams(vmem_limit_bytes=VMEM_LIMIT),
        name="pack_kv",
    )(heads, lengths, keys, values)


def attention_kernel(count, scalars_ref, q_ref, *refs):
    pieces, (out_ref, keys, values, bias) = refs[:count], refs[count:]
    tokens = q_ref.shape[0]
    half = tokens // 2
    slots = (pieces[0].shape[0] - FLAG_ROWS) // 2
    start, core = scalars_ref[0], scalars_ref[1]
    token = lax.broadcasted_iota(jnp.int32, (tokens, slots), 0) + start
    lane = lax.broadcasted_iota(jnp.int32, (tokens, slots), 1)
    lane_row = lax.broadcasted_iota(jnp.int32, (1, slots), 1).astype(jnp.float32)
    for i, piece in enumerate(pieces):
        rows = slice(i * slots, (i + 1) * slots)
        keys[rows, :] = piece[:slots, :]
        values[rows, :] = piece[slots : 2 * slots, :]
        length = piece[2 * slots :, :].astype(jnp.float32)[:1, :slots]
        dead = jnp.where(lane_row < length, 0.0, -1e30)
        seen = lane + scalars_ref[2 + i] * slots <= token
        bias[:, rows] = jnp.where(seen, dead, -1e30)
    factor = HEAD_DIM ** (-0.5) * math.log2(math.e)
    for head in range(q_ref.shape[1] // HEAD_DIM):
        cols = slice(head * HEAD_DIM, (head + 1) * HEAD_DIM)
        for block in range(2):
            rows = slice(block * half, (block + 1) * half)
            scores = lax.dot_general(
                q_ref[rows, cols],
                keys[...],
                (((1,), (1,)), ((), ())),
                preferred_element_type=jnp.float32,
            )
            scores = scores + bias[rows, :]
            top = jnp.max(scores, axis=-1, keepdims=True)
            weights = jnp.exp2((scores - top) * factor)
            total = jnp.sum(weights, axis=-1, keepdims=True)
            mixed = jnp.dot(
                weights.astype(jnp.bfloat16), values[...], preferred_element_type=jnp.float32
            )
            place = pl.ds(pl.multiple_of((core ^ block) * half, half), half)
            out_ref[place, cols] = (mixed / total).astype(jnp.bfloat16)


def attention(scalars, queries, pieces):
    tokens, width = queries.shape
    slots = (pieces[0].shape[0] - FLAG_ROWS) // 2
    count = len(pieces)
    smem = pl.BlockSpec(memory_space=pltpu.SMEM)
    vmem = pl.BlockSpec(memory_space=pltpu.VMEM)
    return pl.pallas_call(
        functools.partial(attention_kernel, count),
        out_shape=jax.ShapeDtypeStruct((tokens, width), jnp.bfloat16),
        in_specs=[smem] + [vmem] * (1 + count),
        out_specs=vmem,
        scratch_shapes=[
            pltpu.VMEM((count * slots, HEAD_DIM), jnp.bfloat16),
            pltpu.VMEM((count * slots, HEAD_DIM), jnp.bfloat16),
            pltpu.VMEM((tokens, count * slots), jnp.float32),
        ],
        compiler_params=pltpu.CompilerParams(vmem_limit_bytes=VMEM_LIMIT),
        cost_estimate=pl.CostEstimate(
            flops=4 * tokens * width * count * slots,
            bytes_accessed=4 * tokens * width + 4 * count * slots * HEAD_DIM,
            transcendentals=tokens * count * slots * (width // HEAD_DIM),
        ),
        name="attention",
    )(scalars, queries, *pieces)


def in_order(kernel, ins, outs):
    def body(*refs):
        inputs, rest = refs[:ins], refs[ins + 1 :]
        kernel(*inputs, *rest[:outs], *rest[outs + 1 :])
        rest[outs][...] = jnp.zeros_like(rest[outs])

    return body


def call(kernel, turn, args, in_specs, out_shapes, out_specs, name, scratch=(), aliases=None):
    turn_shape = jax.ShapeDtypeStruct((8, 128), jnp.float32)
    *results, turn = pl.pallas_call(
        in_order(kernel, len(args), len(out_shapes)),
        out_shape=[*out_shapes, turn_shape],
        in_specs=[*in_specs, pl.BlockSpec(memory_space=pl.ANY)],
        out_specs=[*out_specs, VMEM],
        scratch_shapes=list(scratch),
        input_output_aliases=aliases or {},
        compiler_params=pltpu.CompilerParams(vmem_limit_bytes=VMEM_LIMIT),
        cost_estimate=pl.CostEstimate(flops=0, bytes_accessed=1 << 17, transcendentals=0),
        name=name,
    )(*args, turn)
    return results, turn


VMEM = pl.BlockSpec(memory_space=pltpu.VMEM)
SMEM = pl.BlockSpec(memory_space=pltpu.SMEM)
ANY = pl.BlockSpec(memory_space=pl.ANY)


def project_kernel(bases, width, where_ref, a_ref, w_ref, *refs):
    outs, (buffer, sems) = refs[:-2], refs[-2:]
    half = a_ref.shape[0] // 2
    side = where_ref[1]
    tile = min(width, BLOCK_COLS)
    blocks = [
        (number, part, i)
        for number in range(len(bases))
        for part in range(2)
        for i in range(width // tile)
    ]
    copies = []
    for at, (number, part, i) in enumerate(blocks):
        first = bases[number] + (side ^ (1 - part)) * width + i * tile
        cols = pl.ds(pl.multiple_of(first, tile), tile)
        slot = at % buffer.shape[0]
        copies.append(pltpu.make_async_copy(w_ref.at[:, cols], buffer.at[slot], sems.at[slot]))
    for copy in copies[: buffer.shape[0]]:
        copy.start()
    for at, (number, part, i) in enumerate(blocks):
        copies[at].wait()
        product = jnp.dot(
            a_ref[...], buffer[at % buffer.shape[0]], preferred_element_type=jnp.float32
        ).astype(jnp.bfloat16)
        if at + buffer.shape[0] < len(blocks):
            copies[at + buffer.shape[0]].start()
        cols = slice(i * tile, (i + 1) * tile)
        outs[2 * number][part, :, cols] = product[:half]
        outs[2 * number + 1][part, :, cols] = product[half:]


def project(turn, where, attended, weight, bases, width):
    tokens, depth = attended.shape
    out = jax.ShapeDtypeStruct((2, tokens // 2, width), jnp.bfloat16)
    count = 2 * len(bases)
    tile = min(width, BLOCK_COLS)
    slots = min(SLOTS, count * width // tile)
    return call(
        functools.partial(project_kernel, bases, width),
        turn,
        [where, attended, weight],
        [SMEM, VMEM, ANY],
        [out] * count,
        [VMEM] * count,
        "project",
        [pltpu.VMEM((slots, depth, tile), jnp.bfloat16), pltpu.SemaphoreType.DMA((slots,))],
    )


def plus(*terms):
    total = terms[0].astype(jnp.float32)
    for term in terms[1:]:
        total = total + term.astype(jnp.float32)
    return total.astype(jnp.bfloat16)


def leave(where, own, core, out):
    out[...] = plus(own[0], core[0])


def join(where, own, core, beside, out):
    out[...] = plus(own[1], core[1], beside[...])


def inward(where, own, core, beside, near, out):
    out[...] = plus(own[1], core[1], beside[...], near[...])


def middle(where, own, across, out):
    out[...] = plus(own[...], across[...])


def join_and_middle(where, own, core, beside, near, across, out):
    inner = where[2]

    @pl.when(inner == 0)
    def _():
        join(where, own, core, beside, out)

    @pl.when(inner == 1)
    def _():
        middle(where, near, across, out)


def choose(where, near, own, out):
    inner = where[2]

    @pl.when(inner == 0)
    def _():
        out[...] = near[...]

    @pl.when(inner == 1)
    def _():
        out[...] = own[...]


def stack(where, own, beside, out):
    out[0] = own[...]
    out[1] = beside[...]


def tick_kernel(jobs, where_ref, *refs):
    at = sum(len(ins) for _, ins, _ in jobs)
    outs = refs[at:]
    at = 0
    for (job, ins, _), out in zip(jobs, outs):
        job(where_ref, *refs[at : at + len(ins)], out)
        at += len(ins)


def tick(turn, where, jobs):
    arrays = [x for _, ins, _ in jobs for x in ins]
    outs = [jax.ShapeDtypeStruct(shape, jnp.bfloat16) for _, _, shape in jobs]
    return call(
        functools.partial(tick_kernel, jobs),
        turn,
        [where, *arrays],
        [SMEM] + [VMEM] * len(arrays),
        outs,
        [VMEM] * len(outs),
        "tick",
    )


def place_kernel(base, width, where_ref, mine, theirs, *refs):
    out_ref, sems = refs[-2:]
    half = mine.shape[1]
    core, side = where_ref[0], where_ref[1]
    copies = []
    for i in range(4):
        row = pl.multiple_of((core ^ (i // 2)) * half, half)
        col = pl.multiple_of(base + (side ^ (i % 2)) * width, width)
        source = (mine, theirs)[i // 2].at[i % 2]
        copies.append(
            pltpu.make_async_copy(
                source, out_ref.at[pl.ds(row, half), pl.ds(col, width)], sems.at[i]
            )
        )
    for copy in copies:
        copy.start()
    for copy in copies:
        copy.wait()


def place(turn, where, mine, theirs, out, base, shape):
    width = mine.shape[2]
    given = [] if out is None else [out]
    (out,), turn = call(
        functools.partial(place_kernel, base, width),
        turn,
        [where, mine, theirs, *given],
        [SMEM, ANY, ANY] + [ANY] * len(given),
        [jax.ShapeDtypeStruct(shape, jnp.bfloat16)],
        [ANY],
        "place",
        [pltpu.SemaphoreType.DMA((4,))],
        {3: 0} if given else None,
    )
    return out, turn


def shards(devices, queries, keys, values, lengths, start_pos, out_weight):
    slots = keys.shape[0]
    tokens = queries.shape[0]
    columns = out_weight.shape[1]
    local_heads = queries.shape[1] // HEAD_DIM
    chips = devices // 2
    line = chips // 2
    me = lax.axis_index("tensor")
    core, chip = me % 2, me // 2
    side, spot = chip % 2, chip // 2

    def swap(x, bits):
        return lax.ppermute(x, "tensor", [(d, d ^ bits) for d in range(devices)])

    def along(x, pairs):
        perm = [(a * 4 + i, b * 4 + i) for a, b in pairs for i in range(4)]
        return lax.ppermute(x, "tensor", perm)

    others = chip ^ jnp.arange(chips, dtype=jnp.int32)
    heads = others * (2 * local_heads) // GROUP
    packed = pack(heads, lengths, keys, values)
    order = sorted(range(1, chips), reverse=True)
    direct = {0: packed[0]}
    for m in order:
        direct[m] = swap(packed[m], 2 * m)
    pieces, shard_ids = [], []
    for m in [0] + order:
        pieces += [direct[m], swap(direct[m], 1)]
        shard_ids += [2 * others[m] + core, 2 * others[m] + (core ^ 1)]
    scalars = jnp.stack([start_pos[0], core, *shard_ids]).astype(jnp.int32)
    attended = attention(scalars, queries, pieces)

    if line != 4:
        partial_value = jnp.dot(attended, out_weight, preferred_element_type=jnp.float32)
        partial_value = jnp.roll(partial_value.astype(jnp.bfloat16), core * (tokens // 2), axis=0)
        summed = lax.psum_scatter(partial_value, "tensor", scatter_dimension=0, tiled=True)
        return lax.all_gather(summed, "tensor", axis=0, tiled=True)

    width = columns // (2 * CHUNKS)
    inner = (spot == 1) | (spot == 2)
    where = jnp.stack([core, side, inner.astype(jnp.int32)]).astype(jnp.int32)
    shape = (tokens // 2, width)
    chunks = [{"base": 2 * chunk * width} for chunk in range(CHUNKS)]
    turn = jnp.zeros((8, 128), jnp.float32)
    out = None

    def project_some(turn, some):
        results, turn = project(
            turn, where, attended, out_weight, [c["base"] for c in some], width
        )
        for i, c in enumerate(some):
            c["own"] = results[2 * i]
            c["core"] = swap(results[2 * i + 1], 1)
        return turn

    def step(turn, time, lane):
        at = {time - i: c for i, c in enumerate(lane)}
        jobs, after = [], []
        if 0 in at:
            c = at[0]
            jobs.append((leave, [c["own"], c["core"]], shape))
            after.append((c, "beside", lambda x: swap(x, 2)))
        if 2 in at:
            c = at[2]
            jobs.append((inward, [c["own"], c["core"], c["beside"], c["near"]], shape))
            after.append((c, "across", lambda x: along(x, [(1, 2), (2, 1)])))
        early, late = at.get(1), at.get(3)
        if early or late:
            ins = [early["own"], early["core"], early["beside"]] if early else []
            ins += [late["across_sent"], late["across"]] if late else []
            job = join_and_middle if early and late else join if early else middle
            jobs.append((job, ins, shape))
            after.append(((early, late), "near", lambda x: swap(x, 4)))
        if 4 in at:
            c = at[4]
            jobs.append((choose, [c["near"], c["near_sent"]], shape))
            after.append((c, "beside", lambda x: swap(x, 2)))
        if 5 in at:
            c = at[5]
            jobs.append((stack, [c["beside_sent"], c["beside"]], (2, *shape)))
            after.append((c, "theirs", lambda x: swap(x, 1)))
        if not jobs:
            return turn
        results, turn = tick(turn, where, jobs)
        for (owner, key, send), x in zip(after, results):
            got = send(x)
            for c in owner if isinstance(owner, tuple) else (owner,):
                if c is not None:
                    c[key], c[key + "_sent"] = got, x
        return turn

    lanes = [chunks[0::2], chunks[1::2]]
    turn = project_some(turn, chunks[:2])
    for time in range(len(lanes[0]) + 6):
        for lane in lanes:
            turn = step(turn, time, lane)
            if 0 <= time - 6 < len(lane):
                c = lane[time - 6]
                out, turn = place(
                    turn, where, c["theirs_sent"], c["theirs"], out, c["base"], (tokens, columns)
                )
        if time == 0:
            turn = project_some(turn, chunks[2:])
    return out


def solution(mesh):
    in_specs = (
        P("groups", "tensor"),
        P(("groups", "tensor"), None),
        P(("groups", "tensor"), None),
        P(("groups", "tensor")),
        P("groups"),
        P("tensor", None),
    )
    out_specs = P("groups", None)
    return jax.shard_map(
        functools.partial(shards, mesh.shape["tensor"]),
        mesh=mesh,
        in_specs=in_specs,
        out_specs=out_specs,
        check_vma=False,
    )
```

```python
import functools
import math

import jax
import jax.numpy as jnp
from jax import lax
from jax.experimental import pallas as pl
from jax.experimental.pallas import tpu as pltpu
from jax.sharding import PartitionSpec as P

HEADS = 128
KV_HEADS = 8
HEAD_DIM = 128
GROUP = HEADS // KV_HEADS
FLAG_ROWS = 16
CHUNKS = 8
BLOCK_COLS = 512
SLOTS = 8
VMEM_LIMIT = 32 * 1024 * 1024
PACK_VMEM_LIMIT = 56 * 1024 * 1024
ATTENTION_ROWS = 256


def position():
    me = lax.axis_index("tensor")
    core, chip = lax.rem(me, 2), lax.div(me, 2)
    return core, chip, lax.rem(chip, 2), lax.div(chip, 2)


def pack_kernel(local_heads, lengths_ref, q_ref, k_ref, v_ref, q_out, *refs):
    out_refs, sems = refs[:-1], refs[-1]
    slots = k_ref.shape[0]
    _, chip, _, _ = position()
    copies = []
    for m in reversed(range(len(out_refs))):
        head = lax.div((chip ^ m) * (2 * local_heads), GROUP)
        cols = pl.ds(pl.multiple_of(head * HEAD_DIM, HEAD_DIM), HEAD_DIM)
        for i, ref in enumerate((k_ref, v_ref)):
            rows = pl.ds(i * slots, slots)
            copies.append(
                pltpu.make_async_copy(ref.at[:, cols], out_refs[m].at[rows], sems.at[2 * m + i])
            )
            copies[-1].start()
    copies.append(pltpu.make_async_copy(q_ref, q_out, sems.at[2 * len(out_refs)]))
    copies[-1].start()
    length = jnp.full((FLAG_ROWS, HEAD_DIM), lengths_ref[0], jnp.int32)
    length = length.astype(jnp.float32).astype(jnp.bfloat16)
    for out in out_refs:
        out[2 * slots :, :] = length
    for copy in copies:
        copy.wait()


def pack(chips, local_heads, lengths, queries, keys, values):
    slots = keys.shape[0]
    piece = jax.ShapeDtypeStruct((2 * slots + FLAG_ROWS, HEAD_DIM), jnp.bfloat16)
    return pl.pallas_call(
        functools.partial(pack_kernel, local_heads),
        out_shape=[jax.ShapeDtypeStruct(queries.shape, queries.dtype)] + [piece] * chips,
        in_specs=[SMEM, ANY, ANY, ANY],
        out_specs=[VMEM] * (1 + chips),
        scratch_shapes=[pltpu.SemaphoreType.DMA((2 * chips + 1,))],
        compiler_params=pltpu.CompilerParams(vmem_limit_bytes=PACK_VMEM_LIMIT),
        name="pack_kv",
    )(lengths, queries, keys, values)


def bundle_kernel(*refs):
    for i, ref in enumerate(refs[:-1]):
        refs[-1][i] = ref[...]


def bundle(turn, pieces):
    shape = (len(pieces), *pieces[0].shape)
    (out,), turn = call(
        bundle_kernel,
        turn,
        pieces,
        [VMEM] * len(pieces),
        [jax.ShapeDtypeStruct(shape, pieces[0].dtype)],
        [VMEM],
        "bundle",
    )
    return out, turn


def attention_kernel(flip, start_ref, queries, pieces, *refs):
    last = flip == 1
    if last:
        near, near_top, near_total, out_ref, *refs = refs
    else:
        near, near_top, near_total, *refs = refs
    keys, values, bias = refs
    tokens = queries.shape[0]
    half = tokens // 2
    slots = (pieces.shape[1] - FLAG_ROWS) // 2
    core, chip, _, _ = position()
    token = lax.broadcasted_iota(jnp.int32, (tokens, slots), 0) + start_ref[0]
    lane = lax.broadcasted_iota(jnp.int32, (tokens, slots), 1)
    lane_row = lax.broadcasted_iota(jnp.int32, (1, slots), 1).astype(jnp.float32)
    for m in range(pieces.shape[0]):
        rows = slice(m * slots, (m + 1) * slots)
        keys[rows, :] = pieces[m, :slots, :]
        values[rows, :] = pieces[m, slots : 2 * slots, :]
        length = pieces[m, 2 * slots :, :].astype(jnp.float32)[:1, :slots]
        dead = jnp.where(lane_row < length, 0.0, -1e30)
        shard = (chip ^ m) * 2 + (core ^ flip)
        bias[:, rows] = jnp.where(lane + shard * slots <= token, dead, -1e30)
    factor = HEAD_DIM ** (-0.5) * math.log2(math.e)
    for head in range(queries.shape[1] // HEAD_DIM):
        cols = slice(head * HEAD_DIM, (head + 1) * HEAD_DIM)
        for block in range(tokens // ATTENTION_ROWS):
            rows = slice(block * ATTENTION_ROWS, (block + 1) * ATTENTION_ROWS)
            scores = lax.dot_general(
                queries[rows, cols],
                keys[...],
                (((1,), (1,)), ((), ())),
                preferred_element_type=jnp.float32,
            )
            scores = scores + bias[rows, :]
            top = jnp.max(scores, axis=-1, keepdims=True)
            if last:
                top_before = near_top[rows, head : head + 1]
                top = jnp.maximum(top, top_before)
            weights = jnp.exp2((scores - top) * factor)
            total = jnp.sum(weights, axis=-1, keepdims=True)
            mixed = jnp.dot(
                weights.astype(jnp.bfloat16), values[...], preferred_element_type=jnp.float32
            )
            if last:
                shrink = jnp.exp2((top_before - top) * factor)
                total = total + near_total[rows, head : head + 1] * shrink
                mixed = mixed + near[rows, cols] * shrink
                result = (mixed / total).astype(jnp.bfloat16)
                for i in range(0, ATTENTION_ROWS, min(half, ATTENTION_ROWS)):
                    first = block * ATTENTION_ROWS + i
                    first = first + core * jnp.where(first < half, half, -half)
                    place = pl.ds(pl.multiple_of(first, 128), min(half, ATTENTION_ROWS))
                    out_ref[place, cols] = result[i : i + min(half, ATTENTION_ROWS)]
            else:
                near[rows, cols] = mixed
                near_top[rows, head : head + 1] = top
                near_total[rows, head : head + 1] = total


def attention(turn, start_pos, queries, pieces, flip, before=None):
    tokens, width = queries.shape
    count = pieces.shape[0]
    slots = (pieces.shape[1] - FLAG_ROWS) // 2
    heads = width // HEAD_DIM
    last = before is not None
    sums = [
        jax.ShapeDtypeStruct((tokens, width), jnp.float32),
        jax.ShapeDtypeStruct((tokens, heads), jnp.float32),
        jax.ShapeDtypeStruct((tokens, heads), jnp.float32),
    ]
    given = before if last else []
    outs = [jax.ShapeDtypeStruct((tokens, width), jnp.bfloat16)] if last else sums
    return call(
        functools.partial(attention_kernel, flip),
        turn,
        [start_pos, queries, pieces, *given],
        [SMEM] + [VMEM] * (2 + len(given)),
        outs,
        [VMEM] * len(outs),
        "attention_theirs" if last else "attention_mine",
        [
            pltpu.VMEM((count * slots, HEAD_DIM), jnp.bfloat16),
            pltpu.VMEM((count * slots, HEAD_DIM), jnp.bfloat16),
            pltpu.VMEM((tokens, count * slots), jnp.float32),
        ],
        bytes_accessed=1 << 24,
    )


VMEM = pl.BlockSpec(memory_space=pltpu.VMEM)
SMEM = pl.BlockSpec(memory_space=pltpu.SMEM)
ANY = pl.BlockSpec(memory_space=pl.ANY)


def in_order(kernel, ins, outs):
    def body(*refs):
        inputs, rest = refs[:ins], refs[ins + 1 :]
        kernel(*inputs, *rest[:outs], *rest[outs + 1 :])
        rest[outs][...] = jnp.zeros_like(rest[outs])

    return body


def call(kernel, turn, args, in_specs, out_shapes, out_specs, name, scratch=(), aliases=None, bytes_accessed=1 << 17):
    turn_shape = jax.ShapeDtypeStruct((8, 128), jnp.float32)
    *results, turn = pl.pallas_call(
        in_order(kernel, len(args), len(out_shapes)),
        out_shape=[*out_shapes, turn_shape],
        in_specs=[*in_specs, pl.BlockSpec(memory_space=pl.ANY)],
        out_specs=[*out_specs, VMEM],
        scratch_shapes=list(scratch),
        input_output_aliases=aliases or {},
        compiler_params=pltpu.CompilerParams(vmem_limit_bytes=VMEM_LIMIT),
        cost_estimate=pl.CostEstimate(flops=0, bytes_accessed=bytes_accessed, transcendentals=0),
        name=name,
    )(*args, turn)
    return results, turn


def project_kernel(bases, width, a_ref, w_ref, *refs):
    outs, (buffer, sems) = refs[:-2], refs[-2:]
    half = a_ref.shape[0] // 2
    _, _, side, _ = position()
    tile = min(width, BLOCK_COLS)
    blocks = [
        (number, part, i)
        for number in range(len(bases))
        for part in range(2)
        for i in range(width // tile)
    ]
    copies = []
    for at, (number, part, i) in enumerate(blocks):
        first = bases[number] + (side ^ (1 - part)) * width + i * tile
        cols = pl.ds(pl.multiple_of(first, tile), tile)
        slot = at % buffer.shape[0]
        copies.append(pltpu.make_async_copy(w_ref.at[:, cols], buffer.at[slot], sems.at[slot]))
    for copy in copies[: buffer.shape[0]]:
        copy.start()
    for at, (number, part, i) in enumerate(blocks):
        copies[at].wait()
        product = jnp.dot(
            a_ref[...], buffer[at % buffer.shape[0]], preferred_element_type=jnp.float32
        ).astype(jnp.bfloat16)
        if at + buffer.shape[0] < len(blocks):
            copies[at + buffer.shape[0]].start()
        cols = slice(i * tile, (i + 1) * tile)
        outs[4 * number + part][:, cols] = product[:half]
        outs[4 * number + 2 + part][:, cols] = product[half:]


def project(turn, attended, weight, bases, width):
    tokens, depth = attended.shape
    out = jax.ShapeDtypeStruct((tokens // 2, width), jnp.bfloat16)
    count = 4 * len(bases)
    tile = min(width, BLOCK_COLS)
    slots = min(SLOTS, 2 * len(bases) * width // tile)
    return call(
        functools.partial(project_kernel, bases, width),
        turn,
        [attended, weight],
        [VMEM, ANY],
        [out] * count,
        [VMEM] * count,
        "project",
        [pltpu.VMEM((slots, depth, tile), jnp.bfloat16), pltpu.SemaphoreType.DMA((slots,))],
    )


def plus(*terms):
    total = terms[0].astype(jnp.float32)
    for term in terms[1:]:
        total = total + term.astype(jnp.float32)
    return total.astype(jnp.bfloat16)


def leave(own, core, out):
    out[...] = plus(own[...], core[...])


def join(own, core, beside, out):
    out[...] = plus(own[...], core[...], beside[...])


def inward(own, core, beside, near, out):
    out[...] = plus(own[...], core[...], beside[...], near[...])


def middle(own, across, out):
    out[...] = plus(own[...], across[...])


def is_inner():
    _, _, _, spot = position()
    return (spot == 1) | (spot == 2)


def join_and_middle(own, core, beside, near, across, out):
    inner = is_inner()

    @pl.when(jnp.logical_not(inner))
    def _():
        join(own, core, beside, out)

    @pl.when(inner)
    def _():
        middle(near, across, out)


def choose(near, own, out):
    inner = is_inner()

    @pl.when(jnp.logical_not(inner))
    def _():
        out[...] = near[...]

    @pl.when(inner)
    def _():
        out[...] = own[...]


def stack(own, beside, out):
    out[0] = own[...]
    out[1] = beside[...]


def tick_kernel(jobs, *refs):
    at = sum(len(ins) for _, ins, _ in jobs)
    outs = refs[at:]
    at = 0
    for (job, ins, _), out in zip(jobs, outs):
        job(*refs[at : at + len(ins)], out)
        at += len(ins)


def tick(turn, jobs):
    arrays = [x for _, ins, _ in jobs for x in ins]
    outs = [jax.ShapeDtypeStruct(shape, jnp.bfloat16) for _, _, shape in jobs]
    return call(
        functools.partial(tick_kernel, jobs),
        turn,
        arrays,
        [VMEM] * len(arrays),
        outs,
        [VMEM] * len(outs),
        "tick",
    )


def place_kernel(base, width, mine, theirs, *refs):
    out_ref, sems = refs[-2:]
    half = mine.shape[1]
    core, _, side, _ = position()
    copies = []
    for i in range(4):
        row = pl.multiple_of((core ^ (i // 2)) * half, half)
        col = pl.multiple_of(base + (side ^ (i % 2)) * width, width)
        source = (mine, theirs)[i // 2].at[i % 2]
        copies.append(
            pltpu.make_async_copy(
                source, out_ref.at[pl.ds(row, half), pl.ds(col, width)], sems.at[i]
            )
        )
    for copy in copies:
        copy.start()
    for copy in copies:
        copy.wait()


def place(turn, mine, theirs, out, base, shape):
    width = mine.shape[2]
    given = [] if out is None else [out]
    (out,), turn = call(
        functools.partial(place_kernel, base, width),
        turn,
        [mine, theirs, *given],
        [ANY, ANY] + [ANY] * len(given),
        [jax.ShapeDtypeStruct(shape, jnp.bfloat16)],
        [ANY],
        "place",
        [pltpu.SemaphoreType.DMA((4,))],
        {2: 0} if given else None,
    )
    return out, turn


def shards(devices, queries, keys, values, lengths, start_pos, out_weight):
    slots = keys.shape[0]
    tokens = queries.shape[0]
    columns = out_weight.shape[1]
    local_heads = queries.shape[1] // HEAD_DIM
    chips = devices // 2
    line = chips // 2

    def swap(x, bits):
        return lax.ppermute(x, "tensor", [(d, d ^ bits) for d in range(devices)])

    def along(x, pairs):
        perm = [(a * 4 + i, b * 4 + i) for a, b in pairs for i in range(4)]
        return lax.ppermute(x, "tensor", perm)

    turn = jnp.zeros((8, 128), jnp.float32)
    fetched, *packed = pack(chips, local_heads, lengths, queries, keys, values)
    direct = {m: swap(packed[m], 2 * m) if m else packed[0] for m in reversed(range(chips))}
    mine, turn = bundle(turn, [direct[m] for m in range(chips)])
    theirs = swap(mine, 1)
    sums, turn = attention(turn, start_pos, fetched, mine, 0)
    (attended,), turn = attention(turn, start_pos, fetched, theirs, 1, sums)

    if line != 4:
        partial_value = jnp.dot(attended, out_weight, preferred_element_type=jnp.float32)
        partial_value = jnp.roll(partial_value.astype(jnp.bfloat16), position()[0] * (tokens // 2), axis=0)
        summed = lax.psum_scatter(partial_value, "tensor", scatter_dimension=0, tiled=True)
        return lax.all_gather(summed, "tensor", axis=0, tiled=True)

    width = columns // (2 * CHUNKS)
    shape = (tokens // 2, width)
    chunks = [{"base": 2 * chunk * width} for chunk in range(CHUNKS)]
    out = None

    def project_some(turn, some):
        results, turn = project(
            turn, attended, out_weight, [c["base"] for c in some], width
        )
        for i, c in enumerate(some):
            c["own"] = results[4 * i : 4 * i + 2]
            c["core"] = [swap(peer, 1) for peer in results[4 * i + 2 : 4 * i + 4]]
        return turn

    def leave_of(c):
        return (leave, [c["own"][0], c["core"][0]], shape), [c], "beside", lambda x: swap(x, 2)

    def jobs_of(at):
        jobs = []
        if 4 in at:
            c = at[4]
            job = choose, [c["near"], c["near_sent"]], shape
            jobs.append((job, [c], "beside", lambda x: swap(x, 2)))
        early, late = at.get(1), at.get(3)
        if early or late:
            ins = [early["own"][1], early["core"][1], early["beside"]] if early else []
            ins += [late["across_sent"], late["across"]] if late else []
            job = join_and_middle if early and late else join if early else middle
            owners = [c for c in (early, late) if c]
            jobs.append(((job, ins, shape), owners, "near", lambda x: swap(x, 4)))
        if 2 in at:
            c = at[2]
            job = inward, [c["own"][1], c["core"][1], c["beside"], c["near"]], shape
            jobs.append((job, [c], "across", lambda x: along(x, [(1, 2), (2, 1)])))
        if 5 in at:
            c = at[5]
            job = stack, [c["beside_sent"], c["beside"]], (2, *shape)
            jobs.append((job, [c], "theirs", lambda x: swap(x, 1)))
        return jobs

    def run(turn, now):
        if not now:
            return turn
        results, turn = tick(turn, [job for job, _, _, _ in now])
        for (_, owners, key, send), x in zip(now, results):
            got = send(x)
            for c in owners:
                c[key], c[key + "_sent"] = got, x
        return turn

    lanes = [chunks[0::2], chunks[1::2]]
    turn = project_some(turn, chunks[:2])
    for time in range(len(lanes[0]) + 6):
        for lane in lanes:
            turn = run(turn, jobs_of({time - i: c for i, c in enumerate(lane)}))
            if 0 <= time - 6 < len(lane):
                c = lane[time - 6]
                out, turn = place(
                    turn, c["theirs_sent"], c["theirs"], out, c["base"], (tokens, columns)
                )
        for lane in lanes:
            if time < len(lane):
                turn = run(turn, [leave_of(lane[time])])
        some = chunks[2 * time + 2 : 2 * time + 4]
        if some:
            turn = project_some(turn, some)
    return out


def solution(mesh):
    in_specs = (
        P("groups", "tensor"),
        P(("groups", "tensor"), None),
        P(("groups", "tensor"), None),
        P(("groups", "tensor")),
        P("groups"),
        P("tensor", None),
    )
    out_specs = P("groups", None)
    return jax.shard_map(
        functools.partial(shards, mesh.shape["tensor"]),
        mesh=mesh,
        in_specs=in_specs,
        out_specs=out_specs,
        check_vma=False,
    )
```

```python
import functools
import math

import jax
import jax.numpy as jnp
from jax import lax
from jax.experimental import pallas as pl
from jax.experimental.pallas import tpu as pltpu
from jax.sharding import PartitionSpec as P

HEADS = 128
KV_HEADS = 8
HEAD_DIM = 128
GROUP = HEADS // KV_HEADS
FLAG_ROWS = 16
CHUNKS = 8
BLOCK_COLS = 1024
SLOTS = 4
STEP_FLOPS = 3 * 10**9
VMEM_LIMIT = 32 * 1024 * 1024
PACK_VMEM_LIMIT = 56 * 1024 * 1024
A3000000000ENTION_ROWS = 256


def position():
    me = lax.axis_index("tensor")
    core, chip = lax.rem(me, 2), lax.div(me, 2)
    return core, chip, lax.rem(chip, 2), lax.div(chip, 2)


def pack_kernel(local_heads, lengths_ref, q_ref, k_ref, v_ref, q_out, *refs):
    out_refs, sems = refs[:-1], refs[-1]
    slots = k_ref.shape[0]
    _, chip, _, _ = position()
    copies = []
    for m in reversed(range(len(out_refs))):
        head = lax.div((chip ^ m) * (2 * local_heads), GROUP)
        cols = pl.ds(pl.multiple_of(head * HEAD_DIM, HEAD_DIM), HEAD_DIM)
        for i, ref in enumerate((k_ref, v_ref)):
            rows = pl.ds(i * slots, slots)
            copies.append(
                pltpu.make_async_copy(ref.at[:, cols], out_refs[m].at[rows], sems.at[2 * m + i])
            )
            copies[-1].start()
    copies.append(pltpu.make_async_copy(q_ref, q_out, sems.at[2 * len(out_refs)]))
    copies[-1].start()
    length = jnp.full((FLAG_ROWS, HEAD_DIM), lengths_ref[0], jnp.int32)
    length = length.astype(jnp.float32).astype(jnp.bfloat16)
    for out in out_refs:
        out[2 * slots :, :] = length
    for copy in copies:
        copy.wait()


def pack(chips, local_heads, lengths, queries, keys, values):
    slots = keys.shape[0]
    piece = jax.ShapeDtypeStruct((2 * slots + FLAG_ROWS, HEAD_DIM), jnp.bfloat16)
    return pl.pallas_call(
        functools.partial(pack_kernel, local_heads),
        out_shape=[jax.ShapeDtypeStruct(queries.shape, queries.dtype)] + [piece] * chips,
        in_specs=[SMEM, ANY, ANY, ANY],
        out_specs=[VMEM] * (1 + chips),
        scratch_shapes=[pltpu.SemaphoreType.DMA((2 * chips + 1,))],
        compiler_params=pltpu.CompilerParams(vmem_limit_bytes=PACK_VMEM_LIMIT),
        name="pack_kv",
    )(lengths, queries, keys, values)


def bundle_kernel(*refs):
    for i, ref in enumerate(refs[:-1]):
        refs[-1][i] = ref[...]


def bundle(turn, pieces):
    shape = (len(pieces), *pieces[0].shape)
    (out,), turn = call(
        bundle_kernel,
        turn,
        pieces,
        [VMEM] * len(pieces),
        [jax.ShapeDtypeStruct(shape, pieces[0].dtype)],
        [VMEM],
        "bundle",
    )
    return out, turn


def attention_kernel(flip, start_ref, queries, pieces, *refs):
    last = flip == 1
    if last:
        near, near_top, near_total, out_ref, *refs = refs
    else:
        near, near_top, near_total, *refs = refs
    keys, values, bias = refs
    tokens = queries.shape[0]
    half = tokens // 2
    slots = (pieces.shape[1] - FLAG_ROWS) // 2
    core, chip, _, _ = position()
    token = lax.broadcasted_iota(jnp.int32, (tokens, slots), 0) + start_ref[0]
    lane = lax.broadcasted_iota(jnp.int32, (tokens, slots), 1)
    lane_row = lax.broadcasted_iota(jnp.int32, (1, slots), 1).astype(jnp.float32)
    for i in range(pieces.shape[0]):
        m = pieces.shape[0] - 1 - i
        rows = slice(i * slots, (i + 1) * slots)
        keys[rows, :] = pieces[i, :slots, :]
        values[rows, :] = pieces[i, slots : 2 * slots, :]
        length = pieces[i, 2 * slots :, :].astype(jnp.float32)[:1, :slots]
        dead = jnp.where(lane_row < length, 0.0, -1e30)
        shard = (chip ^ m) * 2 + (core ^ flip)
        bias[:, rows] = jnp.where(lane + shard * slots <= token, dead, -1e30)
    factor = HEAD_DIM ** (-0.5) * math.log2(math.e)
    for head in range(queries.shape[1] // HEAD_DIM):
        cols = slice(head * HEAD_DIM, (head + 1) * HEAD_DIM)
        for block in range(tokens // A3000000000ENTION_ROWS):
            rows = slice(block * A3000000000ENTION_ROWS, (block + 1) * A3000000000ENTION_ROWS)
            scores = lax.dot_general(
                queries[rows, cols],
                keys[...],
                (((1,), (1,)), ((), ())),
                preferred_element_type=jnp.float32,
            )
            scores = scores + bias[rows, :]
            top = jnp.max(scores, axis=-1, keepdims=True)
            if last:
                top_before = near_top[rows, head : head + 1]
                top = jnp.maximum(top, top_before)
            weights = jnp.exp2((scores - top) * factor)
            total = jnp.sum(weights, axis=-1, keepdims=True)
            mixed = jnp.dot(
                weights.astype(jnp.bfloat16), values[...], preferred_element_type=jnp.float32
            )
            if last:
                shrink = jnp.exp2((top_before - top) * factor)
                total = total + near_total[rows, head : head + 1] * shrink
                mixed = mixed + near[rows, cols] * shrink
                result = (mixed / total).astype(jnp.bfloat16)
                for i in range(0, A3000000000ENTION_ROWS, min(half, A3000000000ENTION_ROWS)):
                    first = block * A3000000000ENTION_ROWS + i
                    first = first + core * jnp.where(first < half, half, -half)
                    place = pl.ds(pl.multiple_of(first, 128), min(half, A3000000000ENTION_ROWS))
                    out_ref[place, cols] = result[i : i + min(half, A3000000000ENTION_ROWS)]
            else:
                near[rows, cols] = mixed
                near_top[rows, head : head + 1] = top
                near_total[rows, head : head + 1] = total


def attention(turn, start_pos, queries, pieces, flip, before=None):
    tokens, width = queries.shape
    count = pieces.shape[0]
    slots = (pieces.shape[1] - FLAG_ROWS) // 2
    heads = width // HEAD_DIM
    last = before is not None
    sums = [
        jax.ShapeDtypeStruct((tokens, width), jnp.float32),
        jax.ShapeDtypeStruct((tokens, heads), jnp.float32),
        jax.ShapeDtypeStruct((tokens, heads), jnp.float32),
    ]
    given = before if last else []
    outs = [jax.ShapeDtypeStruct((tokens, width), jnp.bfloat16)] if last else sums
    return call(
        functools.partial(attention_kernel, flip),
        turn,
        [start_pos, queries, pieces, *given],
        [SMEM] + [VMEM] * (2 + len(given)),
        outs,
        [VMEM] * len(outs),
        "attention_theirs" if last else "attention_mine",
        [
            pltpu.VMEM((count * slots, HEAD_DIM), jnp.bfloat16),
            pltpu.VMEM((count * slots, HEAD_DIM), jnp.bfloat16),
            pltpu.VMEM((tokens, count * slots), jnp.float32),
        ],
        bytes_accessed=1 << 24,
    )


VMEM = pl.BlockSpec(memory_space=pltpu.VMEM)
SMEM = pl.BlockSpec(memory_space=pltpu.SMEM)
ANY = pl.BlockSpec(memory_space=pl.ANY)


def in_order(kernel, ins, outs):
    def body(*refs):
        inputs, rest = refs[:ins], refs[ins + 1 :]
        kernel(*inputs, *rest[:outs], *rest[outs + 1 :])
        rest[outs][...] = jnp.zeros_like(rest[outs])

    return body


def call(kernel, turn, args, in_specs, out_shapes, out_specs, name, scratch=(), aliases=None, bytes_accessed=1 << 17):
    turn_shape = jax.ShapeDtypeStruct((8, 128), jnp.float32)
    *results, turn = pl.pallas_call(
        in_order(kernel, len(args), len(out_shapes)),
        out_shape=[*out_shapes, turn_shape],
        in_specs=[*in_specs, pl.BlockSpec(memory_space=pl.ANY)],
        out_specs=[*out_specs, VMEM],
        scratch_shapes=list(scratch),
        input_output_aliases=aliases or {},
        compiler_params=pltpu.CompilerParams(vmem_limit_bytes=VMEM_LIMIT),
        cost_estimate=pl.CostEstimate(flops=STEP_FLOPS, bytes_accessed=bytes_accessed, transcendentals=0),
        name=name,
    )(*args, turn)
    return results, turn


def project_kernel(bases, width, a_ref, w_ref, *refs):
    outs, (buffer, sems) = refs[:-2], refs[-2:]
    half = a_ref.shape[0] // 2
    _, _, side, _ = position()
    tile = min(width, BLOCK_COLS)
    blocks = [
        (number, part, i)
        for number in range(len(bases))
        for part in range(2)
        for i in range(width // tile)
    ]
    copies = []
    for at, (number, part, i) in enumerate(blocks):
        first = bases[number] + (side ^ (1 - part)) * width + i * tile
        cols = pl.ds(pl.multiple_of(first, tile), tile)
        slot = at % buffer.shape[0]
        copies.append(pltpu.make_async_copy(w_ref.at[:, cols], buffer.at[slot], sems.at[slot]))
    for copy in copies[: buffer.shape[0]]:
        copy.start()
    for at, (number, part, i) in enumerate(blocks):
        copies[at].wait()
        product = jnp.dot(
            a_ref[...], buffer[at % buffer.shape[0]], preferred_element_type=jnp.float32
        ).astype(jnp.bfloat16)
        if at + buffer.shape[0] < len(blocks):
            copies[at + buffer.shape[0]].start()
        cols = slice(i * tile, (i + 1) * tile)
        outs[4 * number + part][:, cols] = product[:half]
        outs[4 * number + 2 + part][:, cols] = product[half:]


def project(turn, attended, weight, bases, width):
    tokens, depth = attended.shape
    out = jax.ShapeDtypeStruct((tokens // 2, width), jnp.bfloat16)
    count = 4 * len(bases)
    tile = min(width, BLOCK_COLS)
    slots = min(SLOTS, 2 * len(bases) * width // tile)
    return call(
        functools.partial(project_kernel, bases, width),
        turn,
        [attended, weight],
        [VMEM, ANY],
        [out] * count,
        [VMEM] * count,
        "project",
        [pltpu.VMEM((slots, depth, tile), jnp.bfloat16), pltpu.SemaphoreType.DMA((slots,))],
    )


def plus(*terms):
    total = terms[0].astype(jnp.float32)
    for term in terms[1:]:
        total = total + term.astype(jnp.float32)
    return total.astype(jnp.bfloat16)


def leave(own, core, out):
    out[...] = plus(own[...], core[...])


def join(own, core, beside, out):
    out[...] = plus(own[...], core[...], beside[...])


def inward(own, core, beside, near, out):
    out[...] = plus(own[...], core[...], beside[...], near[...])


def middle(own, across, out):
    out[...] = plus(own[...], across[...])


def is_inner():
    _, _, _, spot = position()
    return (spot == 1) | (spot == 2)


def join_and_middle(own, core, beside, near, across, out):
    inner = is_inner()

    @pl.when(jnp.logical_not(inner))
    def _():
        join(own, core, beside, out)

    @pl.when(inner)
    def _():
        middle(near, across, out)


def choose(near, own, out):
    inner = is_inner()

    @pl.when(jnp.logical_not(inner))
    def _():
        out[...] = near[...]

    @pl.when(inner)
    def _():
        out[...] = own[...]


def stack(own, beside, out):
    out[0] = own[...]
    out[1] = beside[...]


def tick_kernel(jobs, *refs):
    at = sum(len(ins) for _, ins, _ in jobs)
    outs = refs[at:]
    at = 0
    for (job, ins, _), out in zip(jobs, outs):
        job(*refs[at : at + len(ins)], out)
        at += len(ins)


def tick(turn, jobs):
    arrays = [x for _, ins, _ in jobs for x in ins]
    outs = [jax.ShapeDtypeStruct(shape, jnp.bfloat16) for _, _, shape in jobs]
    return call(
        functools.partial(tick_kernel, jobs),
        turn,
        arrays,
        [VMEM] * len(arrays),
        outs,
        [VMEM] * len(outs),
        "tick",
    )


def place_kernel(base, width, mine, theirs, *refs):
    out_ref, sems = refs[-2:]
    half = mine.shape[1]
    core, _, side, _ = position()
    copies = []
    for i in range(4):
        row = pl.multiple_of((core ^ (i // 2)) * half, half)
        col = pl.multiple_of(base + (side ^ (i % 2)) * width, width)
        source = (mine, theirs)[i // 2].at[i % 2]
        copies.append(
            pltpu.make_async_copy(
                source, out_ref.at[pl.ds(row, half), pl.ds(col, width)], sems.at[i]
            )
        )
    for copy in copies:
        copy.start()
    for copy in copies:
        copy.wait()


def place(turn, mine, theirs, out, base, shape):
    width = mine.shape[2]
    given = [] if out is None else [out]
    (out,), turn = call(
        functools.partial(place_kernel, base, width),
        turn,
        [mine, theirs, *given],
        [ANY, ANY] + [ANY] * len(given),
        [jax.ShapeDtypeStruct(shape, jnp.bfloat16)],
        [ANY],
        "place",
        [pltpu.SemaphoreType.DMA((4,))],
        {2: 0} if given else None,
    )
    return out, turn


def shards(devices, queries, keys, values, lengths, start_pos, out_weight):
    slots = keys.shape[0]
    tokens = queries.shape[0]
    columns = out_weight.shape[1]
    local_heads = queries.shape[1] // HEAD_DIM
    chips = devices // 2
    line = chips // 2

    def swap(x, bits):
        return lax.ppermute(x, "tensor", [(d, d ^ bits) for d in range(devices)])

    def along(x, pairs):
        perm = [(a * 4 + i, b * 4 + i) for a, b in pairs for i in range(4)]
        return lax.ppermute(x, "tensor", perm)

    turn = jnp.zeros((8, 128), jnp.float32)
    fetched, *packed = pack(chips, local_heads, lengths, queries, keys, values)
    direct = {m: swap(packed[m], 2 * m) if m else packed[0] for m in reversed(range(chips))}
    mine, turn = bundle(turn, [direct[m] for m in reversed(range(chips))])
    theirs = swap(mine, 1)
    sums, turn = attention(turn, start_pos, fetched, mine, 0)
    (attended,), turn = attention(turn, start_pos, fetched, theirs, 1, sums)

    if line != 4:
        partial_value = jnp.dot(attended, out_weight, preferred_element_type=jnp.float32)
        partial_value = jnp.roll(partial_value.astype(jnp.bfloat16), position()[0] * (tokens // 2), axis=0)
        summed = lax.psum_scatter(partial_value, "tensor", scatter_dimension=0, tiled=True)
        return lax.all_gather(summed, "tensor", axis=0, tiled=True)

    width = columns // (2 * CHUNKS)
    shape = (tokens // 2, width)
    chunks = [{"base": 2 * chunk * width} for chunk in range(CHUNKS)]
    out = None

    def project_some(turn, some):
        results, turn = project(
            turn, attended, out_weight, [c["base"] for c in some], width
        )
        for i, c in enumerate(some):
            c["own"] = results[4 * i : 4 * i + 2]
            c["core"] = [swap(peer, 1) for peer in results[4 * i + 2 : 4 * i + 4]]
        return turn

    def leave_of(c):
        return (leave, [c["own"][0], c["core"][0]], shape), [c], "beside", lambda x: swap(x, 2)

    def jobs_of(at):
        jobs = []
        if 4 in at:
            c = at[4]
            job = choose, [c["near"], c["near_sent"]], shape
            jobs.append((job, [c], "beside", lambda x: swap(x, 2)))
        early, late = at.get(1), at.get(3)
        if early or late:
            ins = [early["own"][1], early["core"][1], early["beside"]] if early else []
            ins += [late["across_sent"], late["across"]] if late else []
            job = join_and_middle if early and late else join if early else middle
            owners = [c for c in (early, late) if c]
            jobs.append(((job, ins, shape), owners, "near", lambda x: swap(x, 4)))
        if 2 in at:
            c = at[2]
            job = inward, [c["own"][1], c["core"][1], c["beside"], c["near"]], shape
            jobs.append((job, [c], "across", lambda x: along(x, [(1, 2), (2, 1)])))
        if 5 in at:
            c = at[5]
            job = stack, [c["beside_sent"], c["beside"]], (2, *shape)
            jobs.append((job, [c], "theirs", lambda x: swap(x, 1)))
        return jobs

    def run(turn, now):
        if not now:
            return turn
        results, turn = tick(turn, [job for job, _, _, _ in now])
        for (_, owners, key, send), x in zip(now, results):
            got = send(x)
            for c in owners:
                c[key], c[key + "_sent"] = got, x
        return turn

    lanes = [chunks[0::2], chunks[1::2]]
    turn = project_some(turn, chunks[:1])
    turn = run(turn, [leave_of(chunks[0])])
    turn = project_some(turn, chunks[1:2])
    turn = run(turn, [leave_of(chunks[1])])
    turn = project_some(turn, chunks[2:4])
    for time in range(len(lanes[0]) + 6):
        for lane in lanes:
            turn = run(turn, jobs_of({time - i: c for i, c in enumerate(lane)}))
            if 0 <= time - 6 < len(lane):
                c = lane[time - 6]
                out, turn = place(
                    turn, c["theirs_sent"], c["theirs"], out, c["base"], (tokens, columns)
                )
            if 0 < time < len(lane):
                turn = run(turn, [leave_of(lane[time])])
                if time + 1 < len(lane):
                    turn = project_some(turn, [lane[time + 1]])
    return out


def solution(mesh):
    in_specs = (
        P("groups", "tensor"),
        P(("groups", "tensor"), None),
        P(("groups", "tensor"), None),
        P(("groups", "tensor")),
        P("groups"),
        P("tensor", None),
    )
    out_specs = P("groups", None)
    return jax.shard_map(
        functools.partial(shards, mesh.shape["tensor"]),
        mesh=mesh,
        in_specs=in_specs,
        out_specs=out_specs,
        check_vma=False,
    )
```

```python
import functools
import math

import jax
import jax.numpy as jnp
from jax import lax
from jax.experimental import pallas as pl
from jax.experimental.pallas import tpu as pltpu
from jax.sharding import PartitionSpec as P

HEADS = 128
KV_HEADS = 8
HEAD_DIM = 128
GROUP = HEADS // KV_HEADS
FLAG_ROWS = 16
CHUNKS = 8
BLOCK_COLS = 1024
SLOTS = 4
STEP_FLOPS = 3 * 10**9
VMEM_LIMIT = 32 * 1024 * 1024
PACK_VMEM_LIMIT = 56 * 1024 * 1024
A3000000000ENTION_ROWS = 256


def position():
    me = lax.axis_index("tensor")
    core, chip = lax.rem(me, 2), lax.div(me, 2)
    return core, chip, lax.rem(chip, 2), lax.div(chip, 2)


def pack_kernel(local_heads, lengths_ref, q_ref, k_ref, v_ref, q_out, *refs):
    out_refs, sems = refs[:-1], refs[-1]
    slots = k_ref.shape[0]
    _, chip, _, _ = position()
    copies = []
    for m in reversed(range(len(out_refs))):
        head = lax.div((chip ^ m) * (2 * local_heads), GROUP)
        cols = pl.ds(pl.multiple_of(head * HEAD_DIM, HEAD_DIM), HEAD_DIM)
        for i, ref in enumerate((k_ref, v_ref)):
            rows = pl.ds(i * slots, slots)
            copies.append(
                pltpu.make_async_copy(ref.at[:, cols], out_refs[m].at[rows], sems.at[2 * m + i])
            )
            copies[-1].start()
    copies.append(pltpu.make_async_copy(q_ref, q_out, sems.at[2 * len(out_refs)]))
    copies[-1].start()
    length = jnp.full((FLAG_ROWS, HEAD_DIM), lengths_ref[0], jnp.int32)
    length = length.astype(jnp.float32).astype(jnp.bfloat16)
    for out in out_refs:
        out[2 * slots :, :] = length
    for copy in copies:
        copy.wait()


def pack(chips, local_heads, lengths, queries, keys, values):
    slots = keys.shape[0]
    piece = jax.ShapeDtypeStruct((2 * slots + FLAG_ROWS, HEAD_DIM), jnp.bfloat16)
    return pl.pallas_call(
        functools.partial(pack_kernel, local_heads),
        out_shape=[jax.ShapeDtypeStruct(queries.shape, queries.dtype)] + [piece] * chips,
        in_specs=[SMEM, ANY, ANY, ANY],
        out_specs=[VMEM] * (1 + chips),
        scratch_shapes=[pltpu.SemaphoreType.DMA((2 * chips + 1,))],
        compiler_params=pltpu.CompilerParams(vmem_limit_bytes=PACK_VMEM_LIMIT),
        name="pack_kv",
    )(lengths, queries, keys, values)


def bundle_kernel(*refs):
    for i, ref in enumerate(refs[:-1]):
        refs[-1][i] = ref[...]


def bundle(turn, pieces):
    shape = (len(pieces), *pieces[0].shape)
    (out,), turn = call(
        bundle_kernel,
        turn,
        pieces,
        [VMEM] * len(pieces),
        [jax.ShapeDtypeStruct(shape, pieces[0].dtype)],
        [VMEM],
        "bundle",
    )
    return out, turn


def attention_kernel(flip, start_ref, queries, pieces, *refs):
    last = flip == 1
    if last:
        near, near_top, near_total, out_ref, *refs = refs
    else:
        near, near_top, near_total, *refs = refs
    keys, values, bias = refs
    tokens = queries.shape[0]
    half = tokens // 2
    slots = (pieces.shape[1] - FLAG_ROWS) // 2
    core, chip, _, _ = position()
    token = lax.broadcasted_iota(jnp.int32, (tokens, slots), 0) + start_ref[0]
    lane = lax.broadcasted_iota(jnp.int32, (tokens, slots), 1)
    lane_row = lax.broadcasted_iota(jnp.int32, (1, slots), 1).astype(jnp.float32)
    for i in range(pieces.shape[0]):
        m = pieces.shape[0] - 1 - i
        rows = slice(i * slots, (i + 1) * slots)
        keys[rows, :] = pieces[i, :slots, :]
        values[rows, :] = pieces[i, slots : 2 * slots, :]
        length = pieces[i, 2 * slots :, :].astype(jnp.float32)[:1, :slots]
        dead = jnp.where(lane_row < length, 0.0, -1e30)
        shard = (chip ^ m) * 2 + (core ^ flip)
        bias[:, rows] = jnp.where(lane + shard * slots <= token, dead, -1e30)
    factor = HEAD_DIM ** (-0.5) * math.log2(math.e)
    for head in range(queries.shape[1] // HEAD_DIM):
        cols = slice(head * HEAD_DIM, (head + 1) * HEAD_DIM)
        for block in range(tokens // A3000000000ENTION_ROWS):
            rows = slice(block * A3000000000ENTION_ROWS, (block + 1) * A3000000000ENTION_ROWS)
            scores = lax.dot_general(
                queries[rows, cols],
                keys[...],
                (((1,), (1,)), ((), ())),
                preferred_element_type=jnp.float32,
            )
            scores = scores + bias[rows, :]
            top = jnp.max(scores, axis=-1, keepdims=True)
            if last:
                top_before = near_top[rows, head : head + 1]
                top = jnp.maximum(top, top_before)
            weights = jnp.exp2((scores - top) * factor)
            total = jnp.sum(weights, axis=-1, keepdims=True)
            mixed = jnp.dot(
                weights.astype(jnp.bfloat16), values[...], preferred_element_type=jnp.float32
            )
            if last:
                shrink = jnp.exp2((top_before - top) * factor)
                total = total + near_total[rows, head : head + 1] * shrink
                mixed = mixed + near[rows, cols] * shrink
                result = (mixed / total).astype(jnp.bfloat16)
                for i in range(0, A3000000000ENTION_ROWS, min(half, A3000000000ENTION_ROWS)):
                    first = block * A3000000000ENTION_ROWS + i
                    first = first + core * jnp.where(first < half, half, -half)
                    place = pl.ds(pl.multiple_of(first, 128), min(half, A3000000000ENTION_ROWS))
                    out_ref[place, cols] = result[i : i + min(half, A3000000000ENTION_ROWS)]
            else:
                near[rows, cols] = mixed
                near_top[rows, head : head + 1] = top
                near_total[rows, head : head + 1] = total


def attention(turn, start_pos, queries, pieces, flip, before=None):
    tokens, width = queries.shape
    count = pieces.shape[0]
    slots = (pieces.shape[1] - FLAG_ROWS) // 2
    heads = width // HEAD_DIM
    last = before is not None
    sums = [
        jax.ShapeDtypeStruct((tokens, width), jnp.float32),
        jax.ShapeDtypeStruct((tokens, heads), jnp.float32),
        jax.ShapeDtypeStruct((tokens, heads), jnp.float32),
    ]
    given = before if last else []
    outs = [jax.ShapeDtypeStruct((tokens, width), jnp.bfloat16)] if last else sums
    return call(
        functools.partial(attention_kernel, flip),
        turn,
        [start_pos, queries, pieces, *given],
        [SMEM] + [VMEM] * (2 + len(given)),
        outs,
        [VMEM] * len(outs),
        "attention_theirs" if last else "attention_mine",
        [
            pltpu.VMEM((count * slots, HEAD_DIM), jnp.bfloat16),
            pltpu.VMEM((count * slots, HEAD_DIM), jnp.bfloat16),
            pltpu.VMEM((tokens, count * slots), jnp.float32),
        ],
        bytes_accessed=1 << 24,
    )


VMEM = pl.BlockSpec(memory_space=pltpu.VMEM)
SMEM = pl.BlockSpec(memory_space=pltpu.SMEM)
ANY = pl.BlockSpec(memory_space=pl.ANY)


def in_order(kernel, ins, outs):
    def body(*refs):
        inputs, rest = refs[:ins], refs[ins + 1 :]
        kernel(*inputs, *rest[:outs], *rest[outs + 1 :])
        rest[outs][...] = jnp.zeros_like(rest[outs])

    return body


def call(kernel, turn, args, in_specs, out_shapes, out_specs, name, scratch=(), aliases=None, bytes_accessed=1 << 17):
    turn_shape = jax.ShapeDtypeStruct((8, 128), jnp.float32)
    *results, turn = pl.pallas_call(
        in_order(kernel, len(args), len(out_shapes)),
        out_shape=[*out_shapes, turn_shape],
        in_specs=[*in_specs, pl.BlockSpec(memory_space=pl.ANY)],
        out_specs=[*out_specs, VMEM],
        scratch_shapes=list(scratch),
        input_output_aliases=aliases or {},
        compiler_params=pltpu.CompilerParams(vmem_limit_bytes=VMEM_LIMIT),
        cost_estimate=pl.CostEstimate(flops=STEP_FLOPS, bytes_accessed=bytes_accessed, transcendentals=0),
        name=name,
    )(*args, turn)
    return results, turn


def project_kernel(bases, width, a_ref, w_ref, *refs):
    outs, (buffer, sems) = refs[:-2], refs[-2:]
    half = a_ref.shape[0] // 2
    _, _, side, _ = position()
    tile = min(width, BLOCK_COLS)
    blocks = [
        (number, part, i)
        for number in range(len(bases))
        for part in range(2)
        for i in range(width // tile)
    ]
    copies = []
    for at, (number, part, i) in enumerate(blocks):
        first = bases[number] + (side ^ (1 - part)) * width + i * tile
        cols = pl.ds(pl.multiple_of(first, tile), tile)
        slot = at % buffer.shape[0]
        copies.append(pltpu.make_async_copy(w_ref.at[:, cols], buffer.at[slot], sems.at[slot]))
    for copy in copies[: buffer.shape[0]]:
        copy.start()
    for at, (number, part, i) in enumerate(blocks):
        copies[at].wait()
        product = jnp.dot(
            a_ref[...], buffer[at % buffer.shape[0]], preferred_element_type=jnp.float32
        ).astype(jnp.bfloat16)
        if at + buffer.shape[0] < len(blocks):
            copies[at + buffer.shape[0]].start()
        cols = slice(i * tile, (i + 1) * tile)
        outs[4 * number + part][:, cols] = product[:half]
        outs[4 * number + 2 + part][:, cols] = product[half:]


def project(turn, attended, weight, bases, width):
    tokens, depth = attended.shape
    out = jax.ShapeDtypeStruct((tokens // 2, width), jnp.bfloat16)
    count = 4 * len(bases)
    tile = min(width, BLOCK_COLS)
    slots = min(SLOTS, 2 * len(bases) * width // tile)
    return call(
        functools.partial(project_kernel, bases, width),
        turn,
        [attended, weight],
        [VMEM, ANY],
        [out] * count,
        [VMEM] * count,
        "project",
        [pltpu.VMEM((slots, depth, tile), jnp.bfloat16), pltpu.SemaphoreType.DMA((slots,))],
    )


def plus(*terms):
    total = terms[0].astype(jnp.float32)
    for term in terms[1:]:
        total = total + term.astype(jnp.float32)
    return total.astype(jnp.bfloat16)


def leave(own, core, out):
    out[...] = plus(own[...], core[...])


def join(own, core, beside, out):
    out[...] = plus(own[...], core[...], beside[...])


def inward(own, core, beside, near, out):
    out[...] = plus(own[...], core[...], beside[...], near[...])


def middle(own, across, out):
    out[...] = plus(own[...], across[...])


def is_inner():
    _, _, _, spot = position()
    return (spot == 1) | (spot == 2)


def join_and_middle(own, core, beside, near, across, out):
    inner = is_inner()

    @pl.when(jnp.logical_not(inner))
    def _():
        join(own, core, beside, out)

    @pl.when(inner)
    def _():
        middle(near, across, out)


def choose(near, own, out):
    inner = is_inner()

    @pl.when(jnp.logical_not(inner))
    def _():
        out[...] = near[...]

    @pl.when(inner)
    def _():
        out[...] = own[...]


def stack(own, beside, out):
    out[0] = own[...]
    out[1] = beside[...]


def tick_kernel(jobs, *refs):
    at = sum(len(ins) for _, ins, _ in jobs)
    outs = refs[at:]
    at = 0
    for (job, ins, _), out in zip(jobs, outs):
        job(*refs[at : at + len(ins)], out)
        at += len(ins)


def tick(turn, jobs):
    arrays = [x for _, ins, _ in jobs for x in ins]
    outs = [jax.ShapeDtypeStruct(shape, jnp.bfloat16) for _, _, shape in jobs]
    return call(
        functools.partial(tick_kernel, jobs),
        turn,
        arrays,
        [VMEM] * len(arrays),
        outs,
        [VMEM] * len(outs),
        "tick",
    )


def place_kernel(base, width, mine, theirs, *refs):
    out_ref, sems = refs[-2:]
    half = mine.shape[1]
    core, _, side, _ = position()
    copies = []
    for i in range(4):
        row = pl.multiple_of((core ^ (i // 2)) * half, half)
        col = pl.multiple_of(base + (side ^ (i % 2)) * width, width)
        source = (mine, theirs)[i // 2].at[i % 2]
        copies.append(
            pltpu.make_async_copy(
                source, out_ref.at[pl.ds(row, half), pl.ds(col, width)], sems.at[i]
            )
        )
    for copy in copies:
        copy.start()
    for copy in copies:
        copy.wait()


def place(turn, mine, theirs, out, base, shape):
    width = mine.shape[2]
    given = [] if out is None else [out]
    (out,), turn = call(
        functools.partial(place_kernel, base, width),
        turn,
        [mine, theirs, *given],
        [ANY, ANY] + [ANY] * len(given),
        [jax.ShapeDtypeStruct(shape, jnp.bfloat16)],
        [ANY],
        "place",
        [pltpu.SemaphoreType.DMA((4,))],
        {2: 0} if given else None,
    )
    return out, turn


def shards(devices, queries, keys, values, lengths, start_pos, out_weight):
    slots = keys.shape[0]
    tokens = queries.shape[0]
    columns = out_weight.shape[1]
    local_heads = queries.shape[1] // HEAD_DIM
    chips = devices // 2
    line = chips // 2

    def swap(x, bits):
        return lax.ppermute(x, "tensor", [(d, d ^ bits) for d in range(devices)])

    def along(x, pairs):
        perm = [(a * 4 + i, b * 4 + i) for a, b in pairs for i in range(4)]
        return lax.ppermute(x, "tensor", perm)

    turn = jnp.zeros((8, 128), jnp.float32)
    fetched, *packed = pack(chips, local_heads, lengths, queries, keys, values)
    direct = {m: swap(packed[m], 2 * m) if m else packed[0] for m in reversed(range(chips))}
    mine, turn = bundle(turn, [direct[m] for m in reversed(range(chips))])
    theirs = swap(mine, 1)
    sums, turn = attention(turn, start_pos, fetched, mine, 0)
    (attended,), turn = attention(turn, start_pos, fetched, theirs, 1, sums)

    if line != 4:
        partial_value = jnp.dot(attended, out_weight, preferred_element_type=jnp.float32)
        partial_value = jnp.roll(partial_value.astype(jnp.bfloat16), position()[0] * (tokens // 2), axis=0)
        summed = lax.psum_scatter(partial_value, "tensor", scatter_dimension=0, tiled=True)
        return lax.all_gather(summed, "tensor", axis=0, tiled=True)

    width = columns // (2 * CHUNKS)
    shape = (tokens // 2, width)
    chunks = [{"base": 2 * chunk * width} for chunk in range(CHUNKS)]
    out = None

    def project_some(turn, some):
        results, turn = project(
            turn, attended, out_weight, [c["base"] for c in some], width
        )
        for i, c in enumerate(some):
            c["own"] = results[4 * i : 4 * i + 2]
            c["core"] = [swap(peer, 1) for peer in results[4 * i + 2 : 4 * i + 4]]
        return turn

    def leave_of(c):
        return (leave, [c["own"][0], c["core"][0]], shape), [c], "beside", lambda x: swap(x, 2)

    def jobs_of(at):
        jobs = []
        if 5 in at:
            c = at[5]
            job = stack, [c["beside_sent"], c["beside"]], (2, *shape)
            jobs.append((job, [c], "theirs", lambda x: swap(x, 1)))
        if 4 in at:
            c = at[4]
            job = choose, [c["near"], c["near_sent"]], shape
            jobs.append((job, [c], "beside", lambda x: swap(x, 2)))
        if 2 in at:
            c = at[2]
            job = inward, [c["own"][1], c["core"][1], c["beside"], c["near"]], shape
            jobs.append((job, [c], "across", lambda x: along(x, [(1, 2), (2, 1)])))
        early, late = at.get(1), at.get(3)
        if early or late:
            ins = [early["own"][1], early["core"][1], early["beside"]] if early else []
            ins += [late["across_sent"], late["across"]] if late else []
            job = join_and_middle if early and late else join if early else middle
            owners = [c for c in (early, late) if c]
            jobs.append(((job, ins, shape), owners, "near", lambda x: swap(x, 4)))
        return jobs

    def run(turn, now):
        if not now:
            return turn
        results, turn = tick(turn, [job for job, _, _, _ in now])
        for (_, owners, key, send), x in zip(now, results):
            got = send(x)
            for c in owners:
                c[key], c[key + "_sent"] = got, x
        return turn

    lanes = [chunks[0::2], chunks[1::2]]
    turn = project_some(turn, chunks[:1])
    turn = run(turn, [leave_of(chunks[0])])
    turn = project_some(turn, chunks[1:2])
    turn = run(turn, [leave_of(chunks[1])])
    turn = project_some(turn, chunks[2:4])
    for time in range(len(lanes[0]) + 6):
        for lane in lanes:
            turn = run(turn, jobs_of({time - i: c for i, c in enumerate(lane)}))
            if 0 <= time - 6 < len(lane):
                c = lane[time - 6]
                out, turn = place(
                    turn, c["theirs_sent"], c["theirs"], out, c["base"], (tokens, columns)
                )
            if 0 < time < len(lane):
                turn = run(turn, [leave_of(lane[time])])
                if time + 1 < len(lane):
                    turn = project_some(turn, [lane[time + 1]])
    return out


def solution(mesh):
    in_specs = (
        P("groups", "tensor"),
        P(("groups", "tensor"), None),
        P(("groups", "tensor"), None),
        P(("groups", "tensor")),
        P("groups"),
        P("tensor", None),
    )
    out_specs = P("groups", None)
    return jax.shard_map(
        functools.partial(shards, mesh.shape["tensor"]),
        mesh=mesh,
        in_specs=in_specs,
        out_specs=out_specs,
        check_vma=False,
    )
```
